32 devices in a mesh: ctx: 8 (over z, y), fsdp: 4 (over x, core).
Axes of the slice: x: 2, y: 2, z: 4, core: 2. Of those that a mesh axis runs over, the one named last changes fastest.
Arguments:
- inputs: bfloat16 [2, 2048, 1024], P(None, ('ctx', 'fsdp')), may hold values from -6 to 6
- attn_gain: bfloat16 [1024], P('fsdp'), may hold values from 0.5 to 1.5
- attn_proj: bfloat16 [1024, 3072], P('fsdp'), may hold values from -0.1875 to 0.1875
- attn_out: bfloat16 [1024, 1024], P('fsdp'), may hold values from -6 to 6
- mlp_gain: bfloat16 [1024], P('fsdp'), may hold values from 0.5 to 1.5
- mlp_in: bfloat16 [1024, 5248], P('fsdp'), may hold values from -0.1875 to 0.1875
- mlp_out: bfloat16 [2624, 1024], P('fsdp'), may hold values from -0.125 to 0.125
- cotangent: bfloat16 [2, 2048, 1024], P(None, ('ctx', 'fsdp')), may hold values from -6 to 6
Outputs:
- outputs: bfloat16 [2, 2048, 1024], P(None, ('ctx', 'fsdp'))
- input_grad: float32 [2, 2048, 1024], P(None, ('ctx', 'fsdp'))
- attn_gain_grad: float32 [1024], P('fsdp')
- attn_proj_grad: float32 [1024, 3072], P('fsdp')
- attn_out_grad: float32 [1024, 1024], P('fsdp')
- mlp_gain_grad: float32 [1024], P('fsdp')
- mlp_in_grad: float32 [1024, 5248], P('fsdp')
- mlp_out_grad: float32 [2624, 1024], P('fsdp')
The draws below stay inside these ranges and needn't reach their ends.
All inputs are finite; a program needn't handle non-finite values.
Results may differ from the reference program's by a relative error of at most 0.02.
Values may be sent and summed in bfloat16 or wider, within the bound.
A program may use at most 768 MiB of HBM per device.

```python
import jax
import jax.numpy as jnp
from jax import lax

D = 1024
HEADS = 16
HEAD_DIM = 64
FF = 2624
SEQS = 2
LEN = 2048


def block_levels(rng, extent, shards, smallest, top_value):
    gain = 1.0
    for dim, shards_of in shards:
        heights = jax.random.uniform(jax.random.fold_in(jax.random.fold_in(rng, 6), dim), (shards_of,), jnp.float32, smallest / len(shards), top_value / len(shards))
        gain = gain * jnp.repeat(jnp.exp(heights), extent[dim] // shards_of).reshape((-1,) + (1,) * (len(extent) - 1 - dim))
    return gain


def scatter_about(own_key, dims, width, reach, shards=(), kind=jnp.bfloat16):
    entries = jax.random.normal(own_key, dims, jnp.float32) * width
    if len(shards) > 0:
        entries = block_levels(own_key, dims, shards, -0.22, 0.18) * entries
    return jnp.clip(entries, min=-reach, max=reach).astype(kind)


def setup_inputs(seed: int = 0) -> dict:
    key_list = jax.random.split(jax.random.key(seed), 9)
    inputs = scatter_about(key_list[0], (SEQS, LEN, D), 1.0, 6.0, ((1, 32),))
    attn_gain = jnp.clip(1.0 + 0.1 * jax.random.normal(key_list[1], (D,), jnp.float32), 0.5, 1.5).astype(jnp.bfloat16)
    attn_proj = scatter_about(key_list[2], (D, 3 * D), D ** -0.5, 0.1875, ((0, 4),))
    attn_out = scatter_about(key_list[3], (D, D), (max(1, 3 * D // LEN)) ** -0.5, 6.0, ((0, 4),))
    mlp_gain = jnp.clip(1.0 + 0.1 * jax.random.normal(key_list[4], (D,), jnp.float32), 0.5, 1.5).astype(jnp.bfloat16)
    mlp_in = scatter_about(key_list[5], (D, 2 * FF), D ** -0.5, 0.1875, ((0, 4),))
    mlp_out = scatter_about(key_list[6], (FF, D), FF ** -0.5, 0.125, ((0, 4),))
    cotangent = scatter_about(key_list[7], (SEQS, LEN, D), 1.0, 6.0, ((1, 32),))
    return dict(inputs=inputs, attn_gain=attn_gain, attn_proj=attn_proj, attn_out=attn_out, mlp_gain=mlp_gain, mlp_in=mlp_in, mlp_out=mlp_out, cotangent=cotangent)


eps = 1e-05
rope_base = 160000.0
highest = lax.Precision.HIGHEST

@jax.custom_vjp
def low(v):
    return lax.optimization_barrier(v.astype(jnp.bfloat16)).astype(jnp.float32)

@jax.custom_vjp
def low_back(v):
    return v

def low_keep(v):
    return (low(v), None)

def low_pass(kept, grad):
    return (grad,)

def back_keep(v):
    return (v, None)

def back_low(kept, grad):
    return (low(grad),)
low.defvjp(low_keep, low_pass)
low_back.defvjp(back_keep, back_low)

def layer_norm(values, norm_gain):
    center = lax.optimization_barrier(jnp.mean(values, axis=-1, keepdims=True))
    centred = values - center
    spread = lax.optimization_barrier(jnp.mean(centred * centred, axis=-1, keepdims=True))
    return centred * lax.rsqrt(spread + eps) * norm_gain

def rotate(values, cos_table, sin_table):
    halfway = values.shape[-1] // 2
    turned = jnp.concatenate([-values[..., halfway:], values[..., :halfway]], axis=-1)
    return values * cos_table + turned * sin_table

def angles(positions, head_size):
    exponent = jnp.arange(0, head_size, 2, dtype=jnp.float32) / head_size
    inverse = rope_base ** (-exponent)
    phases = positions.astype(jnp.float32)[:, None] * inverse[None, :]
    phases = jnp.concatenate([phases, phases], axis=-1)
    return (jnp.cos(phases)[:, None, :], jnp.sin(phases)[:, None, :])

def attention(queries, key_rows, value_rows):
    group_size, length, head_count, head_size = queries.shape
    block_rows = min(512, length)
    scaling = head_size ** (-0.5)
    blocks = queries.reshape(group_size, length // block_rows, block_rows, head_count, head_size).transpose(1, 0, 2, 3, 4)

    def one_block(query_part):
        scores = low_back(jnp.einsum('gqhd,gkhd->ghqk', query_part, key_rows, precision=highest) * scaling)
        weights = low(jax.nn.softmax(scores, axis=-1))
        return jnp.einsum('ghqk,gkhd->gqhd', weights, value_rows, precision=highest)
    outcome = lax.map(jax.checkpoint(one_block), blocks)
    return outcome.transpose(1, 0, 2, 3, 4).reshape(group_size, length, head_count * head_size)

def forward(states, attn_gain, attn_proj, attn_out, mlp_gain, mlp_in, mlp_out):
    group_size, length, model_width = states.shape
    normed = low(layer_norm(states, attn_gain)).reshape(-1, model_width)
    mixed_rows = low_back(jnp.dot(normed, attn_proj, precision=highest))
    mixed_rows = mixed_rows.reshape(group_size, length, 3, HEADS, HEAD_DIM)
    cos_table, sin_table = angles(jnp.arange(length, dtype=jnp.int32), HEAD_DIM)
    queries = low(rotate(mixed_rows[:, :, 0], cos_table, sin_table))
    key_rows = low(rotate(mixed_rows[:, :, 1], cos_table, sin_table))
    value_rows = low(mixed_rows[:, :, 2])
    context = low(low_back(attention(queries, key_rows, value_rows).reshape(-1, model_width)))
    branch = low_back(jnp.dot(context, attn_out, precision=highest))
    middle = states + branch.reshape(group_size, length, model_width)
    normed_two = low(layer_norm(middle, mlp_gain)).reshape(-1, model_width)
    lifted = low_back(jnp.dot(normed_two, mlp_in, precision=highest))
    gate_out = low(jax.nn.gelu(lifted[:, :FF], approximate=False) * lifted[:, FF:])
    return middle + jnp.dot(gate_out, mlp_out, precision=highest).reshape(group_size, length, model_width)

def reference(inputs, attn_gain, attn_proj, attn_out, mlp_gain, mlp_in, mlp_out, cotangent):
    params = (attn_gain.astype(jnp.float32), attn_proj.astype(jnp.float32), attn_out.astype(jnp.float32), mlp_gain.astype(jnp.float32), mlp_in.astype(jnp.float32), mlp_out.astype(jnp.float32))
    group_size = min(SEQS, max(1, 4096 // LEN))
    group_count = SEQS // group_size
    states = inputs.astype(jnp.float32).reshape(group_count, group_size, LEN, D)
    seed_rows = cotangent.astype(jnp.float32).reshape(group_count, group_size, LEN, D)

    def one_group(totals, paired):
        result, pullback = jax.vjp(forward, paired[0], params[0], params[1], params[2], params[3], params[4], params[5])
        gradients = pullback(paired[1])
        totals = tuple((entry + update for entry, update in zip(totals, gradients[1:])))
        return (totals, (result.astype(jnp.bfloat16), gradients[0]))
    zero_sums = tuple((jnp.zeros_like(entry) for entry in params))
    totals, (outputs, input_grad) = lax.scan(one_group, zero_sums, (states, seed_rows))
    return (outputs.reshape(SEQS, LEN, D), input_grad.reshape(SEQS, LEN, D), totals[0], totals[1], totals[2], totals[3], totals[4], totals[5])
```

```python
import functools

import jax
import jax.numpy as jnp
from jax import lax
from jax.experimental import pallas as pl
from jax.experimental.pallas import tpu as pltpu
from jax.sharding import PartitionSpec as P

HEADS = 16
HEAD_DIM = 64


eps = 1e-05
rope_base = 160000.0


def layer_norm(values, norm_gain):
    center = jnp.mean(values, axis=-1, keepdims=True)
    centred = values - center
    spread = jnp.mean(centred * centred, axis=-1, keepdims=True)
    return centred * lax.rsqrt(spread + eps) * norm_gain


def rotate(values, cos_table, sin_table):
    halfway = values.shape[-1] // 2
    turned = jnp.concatenate([-values[..., halfway:], values[..., :halfway]], axis=-1)
    return values * cos_table + turned * sin_table


def unrotate(gradient, cos_table, sin_table):
    halfway = gradient.shape[-1] // 2
    sined = gradient * sin_table
    return gradient * cos_table + jnp.concatenate(
        [sined[..., halfway:], -sined[..., :halfway]], axis=-1
    )


def angles(positions, head_size):
    exponent = jnp.arange(0, head_size, 2, dtype=jnp.float32) / head_size
    inverse = rope_base ** (-exponent)
    phases = positions.astype(jnp.float32)[:, None] * inverse[None, :]
    phases = jnp.concatenate([phases, phases], axis=-1)
    return (jnp.cos(phases)[:, None, :], jnp.sin(phases)[:, None, :])


def gated_unit(lifted):
    hidden_units = lifted.shape[-1] // 2
    return jax.nn.gelu(lifted[..., :hidden_units], approximate=False) * lifted[..., hidden_units:]


def as_heads(flat_rows, head_size):
    return flat_rows.reshape(flat_rows.shape[0], flat_rows.shape[1], -1, head_size)


def empty_state(seq_count, head_count, query_rows, head_size):
    return (
        jnp.full((seq_count, head_count, query_rows), -jnp.inf, jnp.float32),
        jnp.zeros((seq_count, head_count, query_rows), jnp.float32),
        jnp.zeros((seq_count, head_count, query_rows, head_size), jnp.float32),
    )


def forward_step(queries, scaling, state_now, shard_part):
    running_max, denominator, weighted = state_now
    key_part = as_heads(shard_part[0], queries.shape[3])
    value_part = as_heads(shard_part[1], queries.shape[3])
    scores = (
        jnp.einsum("sqhd,skhd->shqk", queries, key_part, preferred_element_type=jnp.float32)
        * scaling
    )
    new_max = jnp.max(scores, axis=-1)
    fading = jnp.exp(running_max - new_max)
    weights = jnp.exp(scores - new_max[..., None])
    denominator = denominator * fading + jnp.sum(weights, axis=-1)
    weighted = weighted * fading[..., None] + jnp.einsum(
        "shqk,skhd->shqd",
        weights.astype(jnp.bfloat16),
        value_part,
        preferred_element_type=jnp.float32,
    )
    return (new_max, denominator, weighted)


def query_step(queries, grad_out, log_total, inner_heads, scaling, shard_part):
    key_part = as_heads(shard_part[0], queries.shape[3])
    value_part = as_heads(shard_part[1], queries.shape[3])
    scores = (
        jnp.einsum("sqhd,skhd->shqk", queries, key_part, preferred_element_type=jnp.float32)
        * scaling
    )
    weights = jnp.exp(scores - log_total[..., None])
    weight_grad = jnp.einsum(
        "sqhd,skhd->shqk", grad_out, value_part, preferred_element_type=jnp.float32
    )
    score_grad = (weights * (weight_grad - inner_heads[..., None])).astype(jnp.bfloat16)
    return jnp.einsum("shqk,skhd->sqhd", score_grad, key_part, preferred_element_type=jnp.float32)


def key_step(key_heads, value_heads, scaling, shard_part):
    head_size = key_heads.shape[3]
    query_part = as_heads(shard_part[0].astype(jnp.bfloat16), head_size)
    grad_part = as_heads(shard_part[1].astype(jnp.bfloat16), head_size)
    log_part = shard_part[2].transpose(0, 2, 1)
    inner_part = shard_part[3].transpose(0, 2, 1)
    scores = (
        jnp.einsum("sqhd,skhd->shqk", query_part, key_heads, preferred_element_type=jnp.float32)
        * scaling
    )
    weights = jnp.exp(scores - log_part[..., None])
    value_grad = jnp.einsum(
        "shqk,sqhd->skhd",
        weights.astype(jnp.bfloat16),
        grad_part,
        preferred_element_type=jnp.float32,
    )
    weight_grad = jnp.einsum(
        "sqhd,skhd->shqk", grad_part, value_heads, preferred_element_type=jnp.float32
    )
    score_grad = (weights * (weight_grad - inner_part[..., None])).astype(jnp.bfloat16)
    key_grad = jnp.einsum(
        "shqk,sqhd->skhd", score_grad, query_part, preferred_element_type=jnp.float32
    )
    return (key_grad, value_grad)


MESH_ID = pl.DeviceIdType.MESH


def exchange_kernel(ctx_count, fsdp_count, x_ref, o_ref, send_sem, recv_sem, own_sem):
    count = ctx_count * fsdp_count
    me = lax.axis_index("ctx") * fsdp_count + lax.axis_index("fsdp")
    barrier = pltpu.get_barrier_semaphore()

    def target(step):
        place = lax.rem(me + step, count)
        return place, (place // fsdp_count, lax.rem(place, fsdp_count))

    def copy_to(step):
        place, device = target(step)
        return pltpu.make_async_remote_copy(
            src_ref=x_ref.at[place],
            dst_ref=o_ref.at[me],
            send_sem=send_sem.at[step],
            recv_sem=recv_sem.at[step],
            device_id=device,
            device_id_type=MESH_ID,
        )

    @pl.loop(1, count)
    def _(step):
        pl.semaphore_signal(barrier, inc=1, device_id=target(step)[1], device_id_type=MESH_ID)

    pl.semaphore_wait(barrier, count - 1)
    own = pltpu.make_async_copy(x_ref.at[me], o_ref.at[me], own_sem)
    own.start()

    @pl.loop(1, count)
    def _(step):
        copy_to(step).start()

    own.wait()

    @pl.loop(1, count)
    def _(step):
        copy_to(step).wait()


def exchange(blocks, ctx_count, fsdp_count, collective_id):
    count = ctx_count * fsdp_count
    return pl.pallas_call(
        functools.partial(exchange_kernel, ctx_count, fsdp_count),
        out_shape=jax.ShapeDtypeStruct(blocks.shape, blocks.dtype),
        in_specs=[pl.BlockSpec(memory_space=pl.ANY)],
        out_specs=pl.BlockSpec(memory_space=pl.ANY),
        scratch_shapes=[
            pltpu.SemaphoreType.DMA((count,)),
            pltpu.SemaphoreType.DMA((count,)),
            pltpu.SemaphoreType.DMA,
        ],
        compiler_params=pltpu.CompilerParams(collective_id=collective_id, has_side_effects=True),
    )(blocks)


def pack(blocks):
    half = blocks.shape[-2] // 2
    return jnp.concatenate([blocks[..., :half, :], blocks[..., half:, :]], axis=-1)


def unpack(blocks):
    half = blocks.shape[-1] // 2
    return jnp.concatenate([blocks[..., :half], blocks[..., half:]], axis=-2)


CONTRACT_LAST = (((1,), (1,)), ((), ()))
CONTRACT_FIRST = (((0,), (0,)), ((), ()))


def attend_kernel(q_ref, k_ref, v_ref, context_ref, log_ref):
    scores = lax.dot_general(
        q_ref[...], k_ref[...], CONTRACT_LAST, preferred_element_type=jnp.float32
    )
    top = jnp.max(scores, axis=-1, keepdims=True)
    weights = jnp.exp(scores - top)
    total = jnp.sum(weights, axis=-1, keepdims=True)
    weighted = jnp.dot(
        weights.astype(jnp.bfloat16), v_ref[...], preferred_element_type=jnp.float32
    )
    context_ref[...] = weighted / total
    log_ref[...] = top + jnp.log(total)


def attend(queries, key_rows, value_rows, block):
    rows, size = queries.shape
    return pl.pallas_call(
        attend_kernel,
        grid=(rows // block,),
        out_shape=(
            jax.ShapeDtypeStruct((rows, size), jnp.float32),
            jax.ShapeDtypeStruct((rows, 1), jnp.float32),
        ),
        in_specs=[
            pl.BlockSpec((block, size), lambda i: (i, 0)),
            pl.BlockSpec((rows, size), lambda i: (0, 0)),
            pl.BlockSpec((rows, size), lambda i: (0, 0)),
        ],
        out_specs=(
            pl.BlockSpec((block, size), lambda i: (i, 0)),
            pl.BlockSpec((block, 1), lambda i: (i, 0)),
        ),
        compiler_params=pltpu.CompilerParams(vmem_limit_bytes=48 * 1024 * 1024),
    )(queries, key_rows, value_rows)


def attend_back_kernel(
    q_ref, k_ref, v_ref, context_ref, log_ref, grad_ref, dq_ref, dk_ref, dv_ref
):
    @pl.when(pl.program_id(0) == 0)
    def _():
        dk_ref[...] = jnp.zeros_like(dk_ref)
        dv_ref[...] = jnp.zeros_like(dv_ref)

    grad = grad_ref[...]
    inner = jnp.sum(grad.astype(jnp.float32) * context_ref[...], axis=-1, keepdims=True)
    scores = lax.dot_general(
        q_ref[...], k_ref[...], CONTRACT_LAST, preferred_element_type=jnp.float32
    )
    probs = jnp.exp(scores - log_ref[...])
    prob_grad = lax.dot_general(
        grad, v_ref[...], CONTRACT_LAST, preferred_element_type=jnp.float32
    )
    score_grad = (probs * (prob_grad - inner)).astype(jnp.bfloat16)
    dv_ref[...] += lax.dot_general(
        probs.astype(jnp.bfloat16), grad, CONTRACT_FIRST, preferred_element_type=jnp.float32
    )
    dk_ref[...] += lax.dot_general(
        score_grad, q_ref[...], CONTRACT_FIRST, preferred_element_type=jnp.float32
    )
    dq_ref[...] = jnp.dot(score_grad, k_ref[...], preferred_element_type=jnp.float32)


def attend_back(queries, key_rows, value_rows, context, log_total, grad, block):
    rows, size = queries.shape
    part = pl.BlockSpec((block, size), lambda i: (i, 0))
    whole = pl.BlockSpec((rows, size), lambda i: (0, 0))
    return pl.pallas_call(
        attend_back_kernel,
        grid=(rows // block,),
        out_shape=(jax.ShapeDtypeStruct((rows, size), jnp.float32),) * 3,
        in_specs=[
            part,
            whole,
            whole,
            part,
            pl.BlockSpec((block, 1), lambda i: (i, 0)),
            part,
        ],
        out_specs=(part, whole, whole),
        compiler_params=pltpu.CompilerParams(vmem_limit_bytes=48 * 1024 * 1024),
    )(queries, key_rows, value_rows, context, log_total, grad)


def by_head_forward(mixed_rows, cos_table, sin_table, scaling):
    seq_count, row_count, _, head_count, head_size = mixed_rows.shape
    ctx_count, fsdp_count = lax.axis_size("ctx"), lax.axis_size("fsdp")
    count = ctx_count * fsdp_count
    queries = rotate(mixed_rows[:, :, 0], cos_table, sin_table).astype(jnp.bfloat16) * scaling
    key_rows = rotate(mixed_rows[:, :, 1], cos_table, sin_table).astype(jnp.bfloat16)
    value_rows = mixed_rows[:, :, 2].astype(jnp.bfloat16)
    to_head = lambda rows: rows.transpose(0, 2, 1, 3).reshape(count, row_count, head_size)
    sent = jnp.concatenate(
        [
            jnp.concatenate([to_head(queries), to_head(key_rows)], axis=-1),
            pack(to_head(value_rows)),
        ],
        axis=1,
    )
    got = exchange(sent, ctx_count, fsdp_count, 1)
    flat = lambda rows: rows.reshape(count * row_count, head_size)
    queries = flat(got[:, :row_count, :head_size])
    key_rows = flat(got[:, :row_count, head_size:])
    value_rows = flat(unpack(got[:, row_count:]))
    context, log_total = attend(queries, key_rows, value_rows, 256)
    back = exchange(
        pack(context.astype(jnp.bfloat16).reshape(count, row_count, head_size)),
        ctx_count,
        fsdp_count,
        2,
    )
    context_low = (
        unpack(back)
        .reshape(seq_count, head_count, row_count, head_size)
        .transpose(0, 2, 1, 3)
        .reshape(seq_count * row_count, head_count * head_size)
    )
    return context_low, (queries, key_rows, value_rows, context, log_total)


def by_head_back(context_grad, saved, scaling):
    seq_count, row_count, head_count, head_size = context_grad.shape
    ctx_count, fsdp_count = lax.axis_size("ctx"), lax.axis_size("fsdp")
    count = ctx_count * fsdp_count
    queries, key_rows, value_rows, context, log_total = saved
    sent = pack(context_grad.transpose(0, 2, 1, 3).reshape(count, row_count, head_size))
    grad = unpack(exchange(sent, ctx_count, fsdp_count, 3)).reshape(count * row_count, head_size)
    query_grad, key_grad, value_grad = attend_back(
        queries, key_rows, value_rows, context, log_total, grad, 256
    )
    cos_all, sin_all = angles(jnp.arange(count * row_count, dtype=jnp.int32), head_size)
    cos_all, sin_all = cos_all[:, 0], sin_all[:, 0]
    query_pre = unrotate(query_grad * scaling, cos_all, sin_all).astype(jnp.bfloat16)
    key_pre = unrotate(key_grad, cos_all, sin_all).astype(jnp.bfloat16)
    split = lambda rows: rows.reshape(count, row_count, head_size)
    sent = jnp.concatenate(
        [
            jnp.concatenate([split(query_pre), split(key_pre)], axis=-1),
            pack(split(value_grad.astype(jnp.bfloat16))),
        ],
        axis=1,
    )
    got = exchange(sent, ctx_count, fsdp_count, 4)
    parts = jnp.stack(
        [got[:, :row_count, :head_size], got[:, :row_count, head_size:], unpack(got[:, row_count:])]
    )
    return (
        parts.reshape(3, seq_count, head_count, row_count, head_size)
        .transpose(1, 3, 0, 2, 4)
        .reshape(seq_count * row_count, 3 * head_count * head_size)
    )


def by_block_forward(mixed_rows, cos_table, sin_table, scaling):
    seq_count, row_count, _, head_count, head_size = mixed_rows.shape
    width = head_count * head_size
    queries = rotate(mixed_rows[:, :, 0], cos_table, sin_table).astype(jnp.bfloat16)
    key_flat = (
        rotate(mixed_rows[:, :, 1], cos_table, sin_table)
        .astype(jnp.bfloat16)
        .reshape(seq_count, row_count, width)
    )
    value_flat = mixed_rows[:, :, 2].astype(jnp.bfloat16).reshape(seq_count, row_count, width)
    key_block, value_block = (
        lax.all_gather(key_flat, "fsdp", axis=1, tiled=True),
        lax.all_gather(value_flat, "fsdp", axis=1, tiled=True),
    )
    start_state = empty_state(seq_count, head_count, row_count, head_size)
    running_max, denominator, weighted = forward_step(
        queries,
        scaling,
        start_state,
        (
            lax.all_gather(key_block, "ctx", axis=1, tiled=True),
            lax.all_gather(value_block, "ctx", axis=1, tiled=True),
        ),
    )
    context = (weighted / denominator[..., None]).transpose(0, 2, 1, 3)
    log_total = running_max + jnp.log(denominator)
    context_low = context.reshape(seq_count * row_count, width).astype(jnp.bfloat16)
    return context_low, (queries, key_block, value_block, context, log_total, cos_table, sin_table)


def by_block_back(context_grad, saved, scaling):
    seq_count, row_count, head_count, head_size = context_grad.shape
    width = head_count * head_size
    queries, key_block, value_block, context, log_total, cos_table, sin_table = saved
    inner = jnp.sum(context_grad.astype(jnp.float32) * context, axis=-1)
    inner_heads = inner.transpose(0, 2, 1)
    log_rows = log_total.transpose(0, 2, 1)
    query_grad = query_step(
        queries,
        context_grad,
        log_total,
        inner_heads,
        scaling,
        (
            lax.all_gather(key_block, "ctx", axis=1, tiled=True),
            lax.all_gather(value_block, "ctx", axis=1, tiled=True),
        ),
    )
    block_len = key_block.shape[1]
    query_wide = queries.reshape(seq_count, row_count, width).astype(jnp.float32)
    grad_wide = context_grad.reshape(seq_count, row_count, width).astype(jnp.float32)
    key_grad, value_grad = key_step(
        as_heads(key_block, head_size),
        as_heads(value_block, head_size),
        scaling,
        (
            lax.all_gather(query_wide, "ctx", axis=1, tiled=True),
            lax.all_gather(grad_wide, "ctx", axis=1, tiled=True),
            lax.all_gather(log_rows, "ctx", axis=1, tiled=True),
            lax.all_gather(inner, "ctx", axis=1, tiled=True),
        ),
    )
    own = lambda grad: lax.psum_scatter(
        grad.reshape(seq_count, block_len, width), "fsdp", scatter_dimension=1, tiled=True
    ).reshape(seq_count, row_count, head_count, head_size)
    query_pre = unrotate(query_grad * scaling, cos_table, sin_table)
    key_pre = unrotate(own(key_grad) * scaling, cos_table, sin_table)
    return (
        jnp.stack([query_pre, key_pre, own(value_grad)], axis=2)
        .reshape(seq_count * row_count, 3 * width)
        .astype(jnp.bfloat16)
    )


def group_rows(rows):
    return lax.all_gather(rows, "fsdp", axis=0, tiled=True)


def group_columns(rows):
    return lax.all_to_all(rows, "fsdp", split_axis=1, concat_axis=0, tiled=True)


def weight_grad(left, right):
    return jnp.einsum("tw,tf->wf", left, right, preferred_element_type=jnp.float32)


def sum_blocks(grads):
    low = lax.psum(tuple(grad.astype(jnp.bfloat16) for grad in grads), "ctx")
    return tuple(grad.astype(jnp.float32) for grad in low)


def on_device(inputs, attn_gain, attn_proj, attn_out, mlp_gain, mlp_in, mlp_out, cotangent):
    seq_count, row_count, model_width = inputs.shape
    head_size = HEAD_DIM
    head_count = HEADS
    scaling = head_size ** (-0.5)
    fsdp_count = lax.axis_size("fsdp")
    fsdp_place = lax.axis_index("fsdp")
    device_count = lax.axis_size("ctx") * fsdp_count
    one_head_each = device_count == seq_count * head_count
    start_row = (lax.axis_index("ctx") * fsdp_count + fsdp_place) * row_count
    cos_table, sin_table = angles(start_row + jnp.arange(row_count, dtype=jnp.int32), head_size)
    tokens = seq_count * row_count
    gains = lax.all_gather(jnp.stack([attn_gain, mlp_gain]), "fsdp", axis=1, tiled=True).astype(
        jnp.float32
    )
    gain_one, gain_two = gains[0], gains[1]
    proj_full, out_full, lift_full, down_full = (
        lax.all_gather(attn_proj, "fsdp", axis=0, tiled=True),
        lax.all_gather(attn_out, "fsdp", axis=0, tiled=True),
        lax.all_gather(mlp_in, "fsdp", axis=0, tiled=True),
        lax.all_gather(mlp_out, "fsdp", axis=0, tiled=True),
    )
    states = inputs.astype(jnp.float32)
    normed, norm_back_one = jax.vjp(layer_norm, states, gain_one)
    normed_low = normed.astype(jnp.bfloat16).reshape(tokens, model_width)
    mixed_rows = jnp.dot(normed_low, proj_full, preferred_element_type=jnp.float32).reshape(
        seq_count, row_count, 3, head_count, head_size
    )
    attention, attention_back = (
        (by_head_forward, by_head_back) if one_head_each else (by_block_forward, by_block_back)
    )
    context_low, saved = attention(mixed_rows, cos_table, sin_table, scaling)
    branch = jnp.dot(context_low, out_full, preferred_element_type=jnp.float32).reshape(
        seq_count, row_count, model_width
    )
    middle = states + branch
    normed_two, norm_back_two = jax.vjp(layer_norm, middle, gain_two)
    normed_two_low = normed_two.astype(jnp.bfloat16).reshape(tokens, model_width)
    lifted = jnp.dot(normed_two_low, lift_full, preferred_element_type=jnp.float32)
    gate_out, gated_back = jax.vjp(gated_unit, lifted)
    gate_low = gate_out.astype(jnp.bfloat16)
    outputs = (
        middle
        + jnp.dot(gate_low, down_full, preferred_element_type=jnp.float32).reshape(
            seq_count, row_count, model_width
        )
    ).astype(jnp.bfloat16)
    seed_rows = cotangent.reshape(tokens, model_width)
    gate_grad = jnp.einsum("td,fd->tf", seed_rows, down_full, preferred_element_type=jnp.float32)
    lifted_grad = gated_back(gate_grad)[0].astype(jnp.bfloat16)
    normed_two_grad = jnp.einsum(
        "tf,wf->tw", lifted_grad, lift_full, preferred_element_type=jnp.float32
    ).reshape(seq_count, row_count, model_width)
    middle_part, gain_two_grad = norm_back_two(normed_two_grad)
    middle_grad = cotangent.astype(jnp.float32) + middle_part
    middle_low = middle_grad.reshape(tokens, model_width).astype(jnp.bfloat16)
    context_grad = (
        jnp.einsum("tv,wv->tw", middle_low, out_full, preferred_element_type=jnp.float32)
        .astype(jnp.bfloat16)
        .reshape(seq_count, row_count, head_count, head_size)
    )
    lift_grad = weight_grad(group_columns(normed_two_low), group_rows(lifted_grad))
    down_grad = weight_grad(group_columns(gate_low), group_rows(seed_rows))
    out_grad = weight_grad(group_columns(context_low), group_rows(middle_low))
    lift_sum, down_sum, out_sum = sum_blocks((lift_grad, down_grad, out_grad))
    mixed_grad = attention_back(context_grad, saved, scaling)
    normed_grad = jnp.einsum(
        "tm,wm->tw", mixed_grad, proj_full, preferred_element_type=jnp.float32
    ).reshape(seq_count, row_count, model_width)
    state_part, gain_one_grad = norm_back_one(normed_grad)
    input_grad = middle_grad + state_part
    proj_grad = weight_grad(group_columns(normed_low), group_rows(mixed_grad))
    (proj_sum,) = sum_blocks((proj_grad,))
    gain_sums = lax.psum(jnp.stack([gain_one_grad, gain_two_grad]), ("ctx", "fsdp"))
    gain_width = attn_gain.shape[0]
    gain_own = lax.dynamic_slice_in_dim(gain_sums, fsdp_place * gain_width, gain_width, axis=1)
    return (
        outputs,
        input_grad,
        gain_own[0],
        proj_sum,
        out_sum,
        gain_own[1],
        lift_sum,
        down_sum,
    )


def solution(mesh):
    in_specs = (
        P(None, ("ctx", "fsdp"), None),
        P("fsdp"),
        P("fsdp", None),
        P("fsdp", None),
        P("fsdp"),
        P("fsdp", None),
        P("fsdp", None),
        P(None, ("ctx", "fsdp"), None),
    )
    out_specs = (
        P(None, ("ctx", "fsdp"), None),
        P(None, ("ctx", "fsdp"), None),
        P("fsdp"),
        P("fsdp", None),
        P("fsdp", None),
        P("fsdp"),
        P("fsdp", None),
        P("fsdp", None),
    )
    return jax.shard_map(
        on_device, mesh=mesh, in_specs=in_specs, out_specs=out_specs, check_vma=False
    )
```

```python
import functools

import jax
import jax.numpy as jnp
from jax import lax
from jax.experimental import pallas as pl
from jax.experimental.pallas import tpu as pltpu
from jax.sharding import PartitionSpec as P

HEADS = 16
HEAD_DIM = 64


eps = 1e-05
rope_base = 160000.0


def layer_norm(values, norm_gain):
    center = jnp.mean(values, axis=-1, keepdims=True)
    centred = values - center
    spread = jnp.mean(centred * centred, axis=-1, keepdims=True)
    return centred * lax.rsqrt(spread + eps) * norm_gain


def rotate(values, cos_table, sin_table):
    halfway = values.shape[-1] // 2
    turned = jnp.concatenate([-values[..., halfway:], values[..., :halfway]], axis=-1)
    return values * cos_table + turned * sin_table


def unrotate(gradient, cos_table, sin_table):
    halfway = gradient.shape[-1] // 2
    sined = gradient * sin_table
    return gradient * cos_table + jnp.concatenate(
        [sined[..., halfway:], -sined[..., :halfway]], axis=-1
    )


def angles(positions, head_size):
    exponent = jnp.arange(0, head_size, 2, dtype=jnp.float32) / head_size
    inverse = rope_base ** (-exponent)
    phases = positions.astype(jnp.float32)[:, None] * inverse[None, :]
    phases = jnp.concatenate([phases, phases], axis=-1)
    return (jnp.cos(phases)[:, None, :], jnp.sin(phases)[:, None, :])


def gated_unit(lifted):
    hidden_units = lifted.shape[-1] // 2
    return jax.nn.gelu(lifted[..., :hidden_units], approximate=False) * lifted[..., hidden_units:]


def as_heads(flat_rows, head_size):
    return flat_rows.reshape(flat_rows.shape[0], flat_rows.shape[1], -1, head_size)


def empty_state(seq_count, head_count, query_rows, head_size):
    return (
        jnp.full((seq_count, head_count, query_rows), -jnp.inf, jnp.float32),
        jnp.zeros((seq_count, head_count, query_rows), jnp.float32),
        jnp.zeros((seq_count, head_count, query_rows, head_size), jnp.float32),
    )


def forward_step(queries, scaling, state_now, shard_part):
    running_max, denominator, weighted = state_now
    key_part = as_heads(shard_part[0], queries.shape[3])
    value_part = as_heads(shard_part[1], queries.shape[3])
    scores = (
        jnp.einsum("sqhd,skhd->shqk", queries, key_part, preferred_element_type=jnp.float32)
        * scaling
    )
    new_max = jnp.max(scores, axis=-1)
    fading = jnp.exp(running_max - new_max)
    weights = jnp.exp(scores - new_max[..., None])
    denominator = denominator * fading + jnp.sum(weights, axis=-1)
    weighted = weighted * fading[..., None] + jnp.einsum(
        "shqk,skhd->shqd",
        weights.astype(jnp.bfloat16),
        value_part,
        preferred_element_type=jnp.float32,
    )
    return (new_max, denominator, weighted)


def query_step(queries, grad_out, log_total, inner_heads, scaling, shard_part):
    key_part = as_heads(shard_part[0], queries.shape[3])
    value_part = as_heads(shard_part[1], queries.shape[3])
    scores = (
        jnp.einsum("sqhd,skhd->shqk", queries, key_part, preferred_element_type=jnp.float32)
        * scaling
    )
    weights = jnp.exp(scores - log_total[..., None])
    weight_grad = jnp.einsum(
        "sqhd,skhd->shqk", grad_out, value_part, preferred_element_type=jnp.float32
    )
    score_grad = (weights * (weight_grad - inner_heads[..., None])).astype(jnp.bfloat16)
    return jnp.einsum("shqk,skhd->sqhd", score_grad, key_part, preferred_element_type=jnp.float32)


def key_step(key_heads, value_heads, scaling, shard_part):
    head_size = key_heads.shape[3]
    query_part = as_heads(shard_part[0].astype(jnp.bfloat16), head_size)
    grad_part = as_heads(shard_part[1].astype(jnp.bfloat16), head_size)
    log_part = shard_part[2].transpose(0, 2, 1)
    inner_part = shard_part[3].transpose(0, 2, 1)
    scores = (
        jnp.einsum("sqhd,skhd->shqk", query_part, key_heads, preferred_element_type=jnp.float32)
        * scaling
    )
    weights = jnp.exp(scores - log_part[..., None])
    value_grad = jnp.einsum(
        "shqk,sqhd->skhd",
        weights.astype(jnp.bfloat16),
        grad_part,
        preferred_element_type=jnp.float32,
    )
    weight_grad = jnp.einsum(
        "sqhd,skhd->shqk", grad_part, value_heads, preferred_element_type=jnp.float32
    )
    score_grad = (weights * (weight_grad - inner_part[..., None])).astype(jnp.bfloat16)
    key_grad = jnp.einsum(
        "shqk,sqhd->skhd", score_grad, query_part, preferred_element_type=jnp.float32
    )
    return (key_grad, value_grad)


MESH_ID = pl.DeviceIdType.MESH


def exchange_kernel(ctx_count, fsdp_count, x_ref, o_ref, send_sem, recv_sem, own_sem):
    count = ctx_count * fsdp_count
    me = lax.axis_index("ctx") * fsdp_count + lax.axis_index("fsdp")
    barrier = pltpu.get_barrier_semaphore()

    def target(step):
        place = lax.rem(me + step, count)
        return place, (place // fsdp_count, lax.rem(place, fsdp_count))

    def copy_to(step):
        place, device = target(step)
        return pltpu.make_async_remote_copy(
            src_ref=x_ref.at[place],
            dst_ref=o_ref.at[me],
            send_sem=send_sem.at[step],
            recv_sem=recv_sem.at[step],
            device_id=device,
            device_id_type=MESH_ID,
        )

    @pl.loop(1, count)
    def _(step):
        pl.semaphore_signal(barrier, inc=1, device_id=target(step)[1], device_id_type=MESH_ID)

    pl.semaphore_wait(barrier, count - 1)
    own = pltpu.make_async_copy(x_ref.at[me], o_ref.at[me], own_sem)
    own.start()

    @pl.loop(1, count)
    def _(step):
        copy_to(step).start()

    own.wait()

    @pl.loop(1, count)
    def _(step):
        copy_to(step).wait()


def exchange(blocks, ctx_count, fsdp_count, collective_id):
    count = ctx_count * fsdp_count
    return pl.pallas_call(
        functools.partial(exchange_kernel, ctx_count, fsdp_count),
        out_shape=jax.ShapeDtypeStruct(blocks.shape, blocks.dtype),
        in_specs=[pl.BlockSpec(memory_space=pl.ANY)],
        out_specs=pl.BlockSpec(memory_space=pl.ANY),
        scratch_shapes=[
            pltpu.SemaphoreType.DMA((count,)),
            pltpu.SemaphoreType.DMA((count,)),
            pltpu.SemaphoreType.DMA,
        ],
        compiler_params=pltpu.CompilerParams(collective_id=collective_id, has_side_effects=True),
    )(blocks)


def gather_kernel(spread, chunks, x_ref, o_ref, send_sem, recv_sem, own_sem):
    ctx, place = lax.axis_index("ctx"), lax.axis_index("fsdp")
    across = lax.rem(place + 2, 4)
    beside = place + 1 - 2 * lax.rem(place, 2)
    half = lax.rem(ctx, 2)
    other_ctx = ctx + 1 - 2 * half
    sibling, partner, neighbour = (ctx, beside), (ctx, across), (other_ctx, place)
    width = x_ref.shape[-1] // (2 * chunks if spread else chunks)
    mine = half * chunks if spread else 0
    theirs = (1 - half) * chunks

    def columns(index):
        return pl.ds(pl.multiple_of(index * width, 128), width)

    def send(src, dst, sem, device):
        return pltpu.make_async_remote_copy(
            src_ref=src,
            dst_ref=dst,
            send_sem=send_sem.at[sem],
            recv_sem=recv_sem.at[sem],
            device_id=device,
            device_id_type=MESH_ID,
        )

    def piece(index):
        return o_ref.at[across, :, columns(index)]

    barrier = pltpu.get_barrier_semaphore()
    partners = (sibling, partner, neighbour) if spread else (sibling, partner)
    for device in partners:
        pl.semaphore_signal(barrier, inc=1, device_id=device, device_id_type=MESH_ID)
    pl.semaphore_wait(barrier, len(partners))
    crossing = [
        send(
            x_ref.at[:, columns(mine + c)],
            o_ref.at[place, :, columns(mine + c)],
            c,
            partner,
        )
        for c in range(chunks)
    ]
    for copy in crossing:
        copy.start()
    started = list(crossing)
    whole = send(x_ref, o_ref.at[place], chunks, sibling)
    whole.start()
    own = pltpu.make_async_copy(x_ref, o_ref.at[place], own_sem)
    own.start()
    turned = []
    for c in range(chunks):
        crossing[c].wait_recv()
        if spread:
            turn = send(piece(mine + c), piece(mine + c), chunks + 1 + c, neighbour)
            turn.start()
            turned.append(turn)
        hand = send(piece(mine + c), piece(mine + c), 2 * chunks + 1 + c, sibling)
        hand.start()
        started.append(hand)
    handed = started[chunks:]
    for c in range(len(turned)):
        turned[c].wait_recv()
        hand = send(piece(theirs + c), piece(theirs + c), 3 * chunks + 1 + c, sibling)
        hand.start()
        handed.append(hand)
    whole.wait_recv()
    own.wait()
    for hand in handed:
        hand.wait_recv()
    for copy in crossing + turned + handed + [whole]:
        copy.wait_send()


def gather(block, spread, chunks, collective_id):
    rows, width = block.shape
    count = 4 * chunks + 1
    return pl.pallas_call(
        functools.partial(gather_kernel, spread, chunks),
        out_shape=jax.ShapeDtypeStruct((4, rows, width), block.dtype),
        in_specs=[pl.BlockSpec(memory_space=pl.ANY)],
        out_specs=pl.BlockSpec(memory_space=pl.ANY),
        scratch_shapes=[
            pltpu.SemaphoreType.DMA((count,)),
            pltpu.SemaphoreType.DMA((count,)),
            pltpu.SemaphoreType.DMA,
        ],
        compiler_params=pltpu.CompilerParams(collective_id=collective_id, has_side_effects=True),
    )(block).reshape(4 * rows, width)


def pack(blocks):
    half = blocks.shape[-2] // 2
    return jnp.concatenate([blocks[..., :half, :], blocks[..., half:, :]], axis=-1)


def unpack(blocks):
    half = blocks.shape[-1] // 2
    return jnp.concatenate([blocks[..., :half], blocks[..., half:]], axis=-2)


CONTRACT_LAST = (((1,), (1,)), ((), ()))
CONTRACT_FIRST = (((0,), (0,)), ((), ()))


def attend_kernel(q_ref, k_ref, v_ref, context_ref, log_ref):
    scores = lax.dot_general(
        q_ref[...], k_ref[...], CONTRACT_LAST, preferred_element_type=jnp.float32
    )
    top = jnp.max(scores, axis=-1, keepdims=True)
    weights = jnp.exp(scores - top)
    total = jnp.sum(weights, axis=-1, keepdims=True)
    weighted = jnp.dot(
        weights.astype(jnp.bfloat16), v_ref[...], preferred_element_type=jnp.float32
    )
    context_ref[...] = weighted / total
    log_ref[...] = top + jnp.log(total)


def attend(queries, key_rows, value_rows, block):
    rows, size = queries.shape
    return pl.pallas_call(
        attend_kernel,
        grid=(rows // block,),
        out_shape=(
            jax.ShapeDtypeStruct((rows, size), jnp.float32),
            jax.ShapeDtypeStruct((rows, 1), jnp.float32),
        ),
        in_specs=[
            pl.BlockSpec((block, size), lambda i: (i, 0)),
            pl.BlockSpec((rows, size), lambda i: (0, 0)),
            pl.BlockSpec((rows, size), lambda i: (0, 0)),
        ],
        out_specs=(
            pl.BlockSpec((block, size), lambda i: (i, 0)),
            pl.BlockSpec((block, 1), lambda i: (i, 0)),
        ),
        compiler_params=pltpu.CompilerParams(vmem_limit_bytes=48 * 1024 * 1024),
    )(queries, key_rows, value_rows)


def attend_back_kernel(
    q_ref, k_ref, v_ref, context_ref, log_ref, grad_ref, dq_ref, dk_ref, dv_ref
):
    @pl.when(pl.program_id(0) == 0)
    def _():
        dk_ref[...] = jnp.zeros_like(dk_ref)
        dv_ref[...] = jnp.zeros_like(dv_ref)

    grad = grad_ref[...]
    inner = jnp.sum(grad.astype(jnp.float32) * context_ref[...], axis=-1, keepdims=True)
    scores = lax.dot_general(
        q_ref[...], k_ref[...], CONTRACT_LAST, preferred_element_type=jnp.float32
    )
    probs = jnp.exp(scores - log_ref[...])
    prob_grad = lax.dot_general(
        grad, v_ref[...], CONTRACT_LAST, preferred_element_type=jnp.float32
    )
    score_grad = (probs * (prob_grad - inner)).astype(jnp.bfloat16)
    dv_ref[...] += lax.dot_general(
        probs.astype(jnp.bfloat16), grad, CONTRACT_FIRST, preferred_element_type=jnp.float32
    )
    dk_ref[...] += lax.dot_general(
        score_grad, q_ref[...], CONTRACT_FIRST, preferred_element_type=jnp.float32
    )
    dq_ref[...] = jnp.dot(score_grad, k_ref[...], preferred_element_type=jnp.float32)


def attend_back(queries, key_rows, value_rows, context, log_total, grad, block):
    rows, size = queries.shape
    part = pl.BlockSpec((block, size), lambda i: (i, 0))
    whole = pl.BlockSpec((rows, size), lambda i: (0, 0))
    return pl.pallas_call(
        attend_back_kernel,
        grid=(rows // block,),
        out_shape=(jax.ShapeDtypeStruct((rows, size), jnp.float32),) * 3,
        in_specs=[
            part,
            whole,
            whole,
            part,
            pl.BlockSpec((block, 1), lambda i: (i, 0)),
            part,
        ],
        out_specs=(part, whole, whole),
        compiler_params=pltpu.CompilerParams(vmem_limit_bytes=48 * 1024 * 1024),
    )(queries, key_rows, value_rows, context, log_total, grad)


def by_head_forward(mixed_rows, cos_table, sin_table, scaling):
    seq_count, row_count, _, head_count, head_size = mixed_rows.shape
    ctx_count, fsdp_count = lax.axis_size("ctx"), lax.axis_size("fsdp")
    count = ctx_count * fsdp_count
    queries = rotate(mixed_rows[:, :, 0], cos_table, sin_table).astype(jnp.bfloat16) * scaling
    key_rows = rotate(mixed_rows[:, :, 1], cos_table, sin_table).astype(jnp.bfloat16)
    value_rows = mixed_rows[:, :, 2].astype(jnp.bfloat16)
    to_head = lambda rows: rows.transpose(0, 2, 1, 3).reshape(count, row_count, head_size)
    sent = jnp.concatenate(
        [
            jnp.concatenate([to_head(queries), to_head(key_rows)], axis=-1),
            pack(to_head(value_rows)),
        ],
        axis=1,
    )
    got = exchange(sent, ctx_count, fsdp_count, 1)
    flat = lambda rows: rows.reshape(count * row_count, head_size)
    queries = flat(got[:, :row_count, :head_size])
    key_rows = flat(got[:, :row_count, head_size:])
    value_rows = flat(unpack(got[:, row_count:]))
    context, log_total = attend(queries, key_rows, value_rows, 256)
    back = exchange(
        pack(context.astype(jnp.bfloat16).reshape(count, row_count, head_size)),
        ctx_count,
        fsdp_count,
        2,
    )
    context_low = (
        unpack(back)
        .reshape(seq_count, head_count, row_count, head_size)
        .transpose(0, 2, 1, 3)
        .reshape(seq_count * row_count, head_count * head_size)
    )
    return context_low, (queries, key_rows, value_rows, context, log_total)


def by_head_back(context_grad, saved, scaling, after):
    seq_count, row_count, head_count, head_size = context_grad.shape
    ctx_count, fsdp_count = lax.axis_size("ctx"), lax.axis_size("fsdp")
    count = ctx_count * fsdp_count
    queries, key_rows, value_rows, context, log_total = saved
    sent = pack(context_grad.transpose(0, 2, 1, 3).reshape(count, row_count, head_size))
    grad = unpack(exchange(sent, ctx_count, fsdp_count, 3)).reshape(count * row_count, head_size)
    query_grad, key_grad, value_grad = attend_back(
        queries, key_rows, value_rows, context, log_total, grad, 256
    )
    cos_all, sin_all = angles(jnp.arange(count * row_count, dtype=jnp.int32), head_size)
    cos_all, sin_all = cos_all[:, 0], sin_all[:, 0]
    query_pre = unrotate(query_grad * scaling, cos_all, sin_all).astype(jnp.bfloat16)
    key_pre = unrotate(key_grad, cos_all, sin_all).astype(jnp.bfloat16)
    split = lambda rows: rows.reshape(count, row_count, head_size)
    sent = jnp.concatenate(
        [
            jnp.concatenate([split(query_pre), split(key_pre)], axis=-1),
            pack(split(value_grad.astype(jnp.bfloat16))),
        ],
        axis=1,
    )
    sent, after = lax.optimization_barrier((sent, after))
    got = exchange(sent, ctx_count, fsdp_count, 4)
    parts = jnp.stack(
        [got[:, :row_count, :head_size], got[:, :row_count, head_size:], unpack(got[:, row_count:])]
    )
    return (
        parts.reshape(3, seq_count, head_count, row_count, head_size)
        .transpose(1, 3, 0, 2, 4)
        .reshape(seq_count * row_count, 3 * head_count * head_size)
    ), after


def by_block_forward(mixed_rows, cos_table, sin_table, scaling):
    seq_count, row_count, _, head_count, head_size = mixed_rows.shape
    width = head_count * head_size
    queries = rotate(mixed_rows[:, :, 0], cos_table, sin_table).astype(jnp.bfloat16)
    key_flat = (
        rotate(mixed_rows[:, :, 1], cos_table, sin_table)
        .astype(jnp.bfloat16)
        .reshape(seq_count, row_count, width)
    )
    value_flat = mixed_rows[:, :, 2].astype(jnp.bfloat16).reshape(seq_count, row_count, width)
    key_block, value_block = (
        lax.all_gather(key_flat, "fsdp", axis=1, tiled=True),
        lax.all_gather(value_flat, "fsdp", axis=1, tiled=True),
    )
    start_state = empty_state(seq_count, head_count, row_count, head_size)
    running_max, denominator, weighted = forward_step(
        queries,
        scaling,
        start_state,
        (
            lax.all_gather(key_block, "ctx", axis=1, tiled=True),
            lax.all_gather(value_block, "ctx", axis=1, tiled=True),
        ),
    )
    context = (weighted / denominator[..., None]).transpose(0, 2, 1, 3)
    log_total = running_max + jnp.log(denominator)
    context_low = context.reshape(seq_count * row_count, width).astype(jnp.bfloat16)
    return context_low, (queries, key_block, value_block, context, log_total, cos_table, sin_table)


def by_block_back(context_grad, saved, scaling, after):
    seq_count, row_count, head_count, head_size = context_grad.shape
    width = head_count * head_size
    queries, key_block, value_block, context, log_total, cos_table, sin_table = saved
    inner = jnp.sum(context_grad.astype(jnp.float32) * context, axis=-1)
    inner_heads = inner.transpose(0, 2, 1)
    log_rows = log_total.transpose(0, 2, 1)
    query_grad = query_step(
        queries,
        context_grad,
        log_total,
        inner_heads,
        scaling,
        (
            lax.all_gather(key_block, "ctx", axis=1, tiled=True),
            lax.all_gather(value_block, "ctx", axis=1, tiled=True),
        ),
    )
    block_len = key_block.shape[1]
    query_wide = queries.reshape(seq_count, row_count, width).astype(jnp.float32)
    grad_wide = context_grad.reshape(seq_count, row_count, width).astype(jnp.float32)
    key_grad, value_grad = key_step(
        as_heads(key_block, head_size),
        as_heads(value_block, head_size),
        scaling,
        (
            lax.all_gather(query_wide, "ctx", axis=1, tiled=True),
            lax.all_gather(grad_wide, "ctx", axis=1, tiled=True),
            lax.all_gather(log_rows, "ctx", axis=1, tiled=True),
            lax.all_gather(inner, "ctx", axis=1, tiled=True),
        ),
    )
    own = lambda grad: lax.psum_scatter(
        grad.reshape(seq_count, block_len, width), "fsdp", scatter_dimension=1, tiled=True
    ).reshape(seq_count, row_count, head_count, head_size)
    query_pre = unrotate(query_grad * scaling, cos_table, sin_table)
    key_pre = unrotate(own(key_grad) * scaling, cos_table, sin_table)
    return (
        jnp.stack([query_pre, key_pre, own(value_grad)], axis=2)
        .reshape(seq_count * row_count, 3 * width)
        .astype(jnp.bfloat16)
    ), after


def group_rows(rows):
    return lax.all_gather(rows, "fsdp", axis=0, tiled=True)


def group_columns(arrays):
    count = lax.axis_size("fsdp")
    widths = [rows.shape[1] // count for rows in arrays]
    sent = jnp.stack(
        [
            jnp.concatenate(
                [rows[:, f * width : (f + 1) * width] for rows, width in zip(arrays, widths)],
                axis=1,
            )
            for f in range(count)
        ]
    )
    got = lax.all_to_all(sent, "fsdp", split_axis=0, concat_axis=0, tiled=True)
    got = got.reshape(-1, sum(widths))
    edges = [sum(widths[:i]) for i in range(len(widths) + 1)]
    return [got[:, edges[i] : edges[i + 1]] for i in range(len(widths))]


def weight_grad(left, right):
    return jnp.einsum("tw,tf->wf", left, right, preferred_element_type=jnp.float32)


def on_device(inputs, attn_gain, attn_proj, attn_out, mlp_gain, mlp_in, mlp_out, cotangent):
    seq_count, row_count, model_width = inputs.shape
    head_size = HEAD_DIM
    head_count = HEADS
    scaling = head_size ** (-0.5)
    fsdp_count = lax.axis_size("fsdp")
    fsdp_place = lax.axis_index("fsdp")
    device_count = lax.axis_size("ctx") * fsdp_count
    one_head_each = device_count == seq_count * head_count
    start_row = (lax.axis_index("ctx") * fsdp_count + fsdp_place) * row_count
    cos_table, sin_table = angles(start_row + jnp.arange(row_count, dtype=jnp.int32), head_size)
    tokens = seq_count * row_count
    gains = lax.all_gather(jnp.stack([attn_gain, mlp_gain]), "fsdp", axis=1, tiled=True).astype(
        jnp.float32
    )
    gain_one, gain_two = gains[0], gains[1]
    ctx_count = lax.axis_size("ctx")
    small = one_head_each and fsdp_count == 4 and ctx_count == 8
    proj_full, out_full, lift_full, down_full = (
        gather(attn_proj, True, 3, 6)
        if small
        else lax.all_gather(attn_proj, "fsdp", axis=0, tiled=True),
        lax.all_gather(attn_out, "fsdp", axis=0, tiled=True),
        lax.all_gather(mlp_in, "fsdp", axis=0, tiled=True),
        lax.all_gather(mlp_out, "fsdp", axis=0, tiled=True),
    )
    states = inputs.astype(jnp.float32)
    normed, norm_back_one = jax.vjp(layer_norm, states, gain_one)
    normed_low = normed.astype(jnp.bfloat16).reshape(tokens, model_width)
    mixed_rows = jnp.dot(normed_low, proj_full, preferred_element_type=jnp.float32).reshape(
        seq_count, row_count, 3, head_count, head_size
    )
    attention, attention_back = (
        (by_head_forward, by_head_back) if one_head_each else (by_block_forward, by_block_back)
    )
    context_low, saved = attention(mixed_rows, cos_table, sin_table, scaling)
    branch = jnp.dot(context_low, out_full, preferred_element_type=jnp.float32).reshape(
        seq_count, row_count, model_width
    )
    middle = states + branch
    normed_two, norm_back_two = jax.vjp(layer_norm, middle, gain_two)
    normed_two_low = normed_two.astype(jnp.bfloat16).reshape(tokens, model_width)
    lifted = jnp.dot(normed_two_low, lift_full, preferred_element_type=jnp.float32)
    gate_out, gated_back = jax.vjp(gated_unit, lifted)
    gate_low = gate_out.astype(jnp.bfloat16)
    outputs = (
        middle
        + jnp.dot(gate_low, down_full, preferred_element_type=jnp.float32).reshape(
            seq_count, row_count, model_width
        )
    ).astype(jnp.bfloat16)
    seed_rows = cotangent.reshape(tokens, model_width)
    gate_grad = jnp.einsum("td,fd->tf", seed_rows, down_full, preferred_element_type=jnp.float32)
    lifted_grad = gated_back(gate_grad)[0].astype(jnp.bfloat16)
    normed_two_grad = jnp.einsum(
        "tf,wf->tw", lifted_grad, lift_full, preferred_element_type=jnp.float32
    ).reshape(seq_count, row_count, model_width)
    middle_part, gain_two_grad = norm_back_two(normed_two_grad)
    middle_grad = cotangent.astype(jnp.float32) + middle_part
    middle_low = middle_grad.reshape(tokens, model_width).astype(jnp.bfloat16)
    context_grad = (
        jnp.einsum("tv,wv->tw", middle_low, out_full, preferred_element_type=jnp.float32)
        .astype(jnp.bfloat16)
        .reshape(seq_count, row_count, head_count, head_size)
    )
    normed_two_part, gate_part, context_part, normed_part = group_columns(
        (normed_two_low, gate_low, context_low, normed_low)
    )
    seed_group = group_rows(seed_rows)
    joined = group_rows(jnp.concatenate([lifted_grad, middle_low], axis=1))
    lift_grad = weight_grad(normed_two_part, joined[:, : lifted_grad.shape[1]])
    out_grad = weight_grad(context_part, joined[:, lifted_grad.shape[1] :])
    down_grad = weight_grad(gate_part, seed_group)
    first_grads = tuple(grad.astype(jnp.bfloat16) for grad in (lift_grad, down_grad, out_grad))
    mixed_grad, first_grads = attention_back(context_grad, saved, scaling, first_grads)
    first_sums = lax.psum(first_grads, "ctx")
    normed_grad = jnp.einsum(
        "tm,wm->tw", mixed_grad, proj_full, preferred_element_type=jnp.float32
    ).reshape(seq_count, row_count, model_width)
    state_part, gain_one_grad = norm_back_one(normed_grad)
    input_grad = middle_grad + state_part
    mixed_group = gather(mixed_grad, False, 4, 7) if small else group_rows(mixed_grad)
    proj_grad = weight_grad(normed_part, mixed_group).astype(jnp.bfloat16)
    proj_grad, first_sums = lax.optimization_barrier((proj_grad, first_sums))
    proj_sum = lax.psum(proj_grad, "ctx").astype(jnp.float32)
    lift_sum, down_sum, out_sum = (total.astype(jnp.float32) for total in first_sums)
    gain_width = attn_gain.shape[0]
    gain_grads = jnp.stack([gain_one_grad, gain_two_grad])
    if small:
        shares = gain_grads.reshape(2, fsdp_count, gain_width).transpose(1, 0, 2)
        shares = jnp.concatenate([shares, jnp.zeros((fsdp_count, 6, gain_width))], axis=1)
        shares = jnp.concatenate([shares] * ctx_count, axis=0)
        gain_own = jnp.sum(exchange(shares, ctx_count, fsdp_count, 5), axis=0)
    else:
        gain_sums = lax.psum(gain_grads, ("ctx", "fsdp"))
        gain_own = lax.dynamic_slice_in_dim(gain_sums, fsdp_place * gain_width, gain_width, axis=1)
    return (
        outputs,
        input_grad,
        gain_own[0],
        proj_sum,
        out_sum,
        gain_own[1],
        lift_sum,
        down_sum,
    )


def solution(mesh):
    in_specs = (
        P(None, ("ctx", "fsdp"), None),
        P("fsdp"),
        P("fsdp", None),
        P("fsdp", None),
        P("fsdp"),
        P("fsdp", None),
        P("fsdp", None),
        P(None, ("ctx", "fsdp"), None),
    )
    out_specs = (
        P(None, ("ctx", "fsdp"), None),
        P(None, ("ctx", "fsdp"), None),
        P("fsdp"),
        P("fsdp", None),
        P("fsdp", None),
        P("fsdp"),
        P("fsdp", None),
        P("fsdp", None),
    )
    return jax.shard_map(
        on_device, mesh=mesh, in_specs=in_specs, out_specs=out_specs, check_vma=False
    )
```

```python
import functools

import jax
import jax.numpy as jnp
from jax import lax
from jax.experimental import pallas as pl
from jax.experimental.pallas import tpu as pltpu
from jax.sharding import PartitionSpec as P

HEADS = 16
HEAD_DIM = 64


eps = 1e-05
rope_base = 160000.0


def layer_norm(values, norm_gain):
    center = jnp.mean(values, axis=-1, keepdims=True)
    centred = values - center
    spread = jnp.mean(centred * centred, axis=-1, keepdims=True)
    return centred * lax.rsqrt(spread + eps) * norm_gain


def rotate(values, cos_table, sin_table):
    halfway = values.shape[-1] // 2
    turned = jnp.concatenate([-values[..., halfway:], values[..., :halfway]], axis=-1)
    return values * cos_table + turned * sin_table


def unrotate(gradient, cos_table, sin_table):
    halfway = gradient.shape[-1] // 2
    sined = gradient * sin_table
    return gradient * cos_table + jnp.concatenate(
        [sined[..., halfway:], -sined[..., :halfway]], axis=-1
    )


def angles(positions, head_size):
    exponent = jnp.arange(0, head_size, 2, dtype=jnp.float32) / head_size
    inverse = rope_base ** (-exponent)
    phases = positions.astype(jnp.float32)[:, None] * inverse[None, :]
    phases = jnp.concatenate([phases, phases], axis=-1)
    return (jnp.cos(phases)[:, None, :], jnp.sin(phases)[:, None, :])


def gated_unit(lifted):
    hidden_units = lifted.shape[-1] // 2
    return jax.nn.gelu(lifted[..., :hidden_units], approximate=False) * lifted[..., hidden_units:]


def as_heads(flat_rows, head_size):
    return flat_rows.reshape(flat_rows.shape[0], flat_rows.shape[1], -1, head_size)


def empty_state(seq_count, head_count, query_rows, head_size):
    return (
        jnp.full((seq_count, head_count, query_rows), -jnp.inf, jnp.float32),
        jnp.zeros((seq_count, head_count, query_rows), jnp.float32),
        jnp.zeros((seq_count, head_count, query_rows, head_size), jnp.float32),
    )


def forward_step(queries, scaling, state_now, shard_part):
    running_max, denominator, weighted = state_now
    key_part = as_heads(shard_part[0], queries.shape[3])
    value_part = as_heads(shard_part[1], queries.shape[3])
    scores = (
        jnp.einsum("sqhd,skhd->shqk", queries, key_part, preferred_element_type=jnp.float32)
        * scaling
    )
    new_max = jnp.max(scores, axis=-1)
    fading = jnp.exp(running_max - new_max)
    weights = jnp.exp(scores - new_max[..., None])
    denominator = denominator * fading + jnp.sum(weights, axis=-1)
    weighted = weighted * fading[..., None] + jnp.einsum(
        "shqk,skhd->shqd",
        weights.astype(jnp.bfloat16),
        value_part,
        preferred_element_type=jnp.float32,
    )
    return (new_max, denominator, weighted)


def query_step(queries, grad_out, log_total, inner_heads, scaling, shard_part):
    key_part = as_heads(shard_part[0], queries.shape[3])
    value_part = as_heads(shard_part[1], queries.shape[3])
    scores = (
        jnp.einsum("sqhd,skhd->shqk", queries, key_part, preferred_element_type=jnp.float32)
        * scaling
    )
    weights = jnp.exp(scores - log_total[..., None])
    weight_grad = jnp.einsum(
        "sqhd,skhd->shqk", grad_out, value_part, preferred_element_type=jnp.float32
    )
    score_grad = (weights * (weight_grad - inner_heads[..., None])).astype(jnp.bfloat16)
    return jnp.einsum("shqk,skhd->sqhd", score_grad, key_part, preferred_element_type=jnp.float32)


def key_step(key_heads, value_heads, scaling, shard_part):
    head_size = key_heads.shape[3]
    query_part = as_heads(shard_part[0].astype(jnp.bfloat16), head_size)
    grad_part = as_heads(shard_part[1].astype(jnp.bfloat16), head_size)
    log_part = shard_part[2].transpose(0, 2, 1)
    inner_part = shard_part[3].transpose(0, 2, 1)
    scores = (
        jnp.einsum("sqhd,skhd->shqk", query_part, key_heads, preferred_element_type=jnp.float32)
        * scaling
    )
    weights = jnp.exp(scores - log_part[..., None])
    value_grad = jnp.einsum(
        "shqk,sqhd->skhd",
        weights.astype(jnp.bfloat16),
        grad_part,
        preferred_element_type=jnp.float32,
    )
    weight_grad = jnp.einsum(
        "sqhd,skhd->shqk", grad_part, value_heads, preferred_element_type=jnp.float32
    )
    score_grad = (weights * (weight_grad - inner_part[..., None])).astype(jnp.bfloat16)
    key_grad = jnp.einsum(
        "shqk,sqhd->skhd", score_grad, query_part, preferred_element_type=jnp.float32
    )
    return (key_grad, value_grad)


MESH_ID = pl.DeviceIdType.MESH


def exchange_kernel(ctx_count, fsdp_count, x_ref, o_ref, send_sem, recv_sem, own_sem):
    count = ctx_count * fsdp_count
    me = lax.axis_index("ctx") * fsdp_count + lax.axis_index("fsdp")
    barrier = pltpu.get_barrier_semaphore()

    def target(step):
        place = lax.rem(me + step, count)
        return place, (place // fsdp_count, lax.rem(place, fsdp_count))

    def copy_to(step):
        place, device = target(step)
        return pltpu.make_async_remote_copy(
            src_ref=x_ref.at[place],
            dst_ref=o_ref.at[me],
            send_sem=send_sem.at[step],
            recv_sem=recv_sem.at[step],
            device_id=device,
            device_id_type=MESH_ID,
        )

    @pl.loop(1, count)
    def _(step):
        pl.semaphore_signal(barrier, inc=1, device_id=target(step)[1], device_id_type=MESH_ID)

    pl.semaphore_wait(barrier, count - 1)
    own = pltpu.make_async_copy(x_ref.at[me], o_ref.at[me], own_sem)
    own.start()

    @pl.loop(1, count)
    def _(step):
        copy_to(step).start()

    own.wait()

    @pl.loop(1, count)
    def _(step):
        copy_to(step).wait()


def exchange(blocks, ctx_count, fsdp_count, collective_id):
    count = ctx_count * fsdp_count
    return pl.pallas_call(
        functools.partial(exchange_kernel, ctx_count, fsdp_count),
        out_shape=jax.ShapeDtypeStruct(blocks.shape, blocks.dtype),
        in_specs=[pl.BlockSpec(memory_space=pl.ANY)],
        out_specs=pl.BlockSpec(memory_space=pl.ANY),
        scratch_shapes=[
            pltpu.SemaphoreType.DMA((count,)),
            pltpu.SemaphoreType.DMA((count,)),
            pltpu.SemaphoreType.DMA,
        ],
        compiler_params=pltpu.CompilerParams(collective_id=collective_id, has_side_effects=True),
    )(blocks)


def gather_kernel(spread, chunks, x_ref, o_ref, send_sem, recv_sem, own_sem):
    ctx, place = lax.axis_index("ctx"), lax.axis_index("fsdp")
    across = lax.rem(place + 2, 4)
    beside = place + 1 - 2 * lax.rem(place, 2)
    half = lax.rem(ctx, 2)
    other_ctx = ctx + 1 - 2 * half
    sibling, partner, neighbour = (ctx, beside), (ctx, across), (other_ctx, place)
    width = x_ref.shape[-1] // (2 * chunks if spread else chunks)
    mine = half * chunks if spread else 0
    theirs = (1 - half) * chunks

    def columns(index):
        return pl.ds(pl.multiple_of(index * width, 128), width)

    def send(src, dst, sem, device):
        return pltpu.make_async_remote_copy(
            src_ref=src,
            dst_ref=dst,
            send_sem=send_sem.at[sem],
            recv_sem=recv_sem.at[sem],
            device_id=device,
            device_id_type=MESH_ID,
        )

    def piece(index):
        return o_ref.at[across, :, columns(index)]

    barrier = pltpu.get_barrier_semaphore()
    partners = (sibling, partner, neighbour) if spread else (sibling, partner)
    for device in partners:
        pl.semaphore_signal(barrier, inc=1, device_id=device, device_id_type=MESH_ID)
    pl.semaphore_wait(barrier, len(partners))
    crossing = [
        send(
            x_ref.at[:, columns(mine + c)],
            o_ref.at[place, :, columns(mine + c)],
            c,
            partner,
        )
        for c in range(chunks)
    ]
    for copy in crossing:
        copy.start()
    started = list(crossing)
    whole = send(x_ref, o_ref.at[place], chunks, sibling)
    whole.start()
    own = pltpu.make_async_copy(x_ref, o_ref.at[place], own_sem)
    own.start()
    turned = []
    for c in range(chunks):
        crossing[c].wait_recv()
        if spread:
            turn = send(piece(mine + c), piece(mine + c), chunks + 1 + c, neighbour)
            turn.start()
            turned.append(turn)
        hand = send(piece(mine + c), piece(mine + c), 2 * chunks + 1 + c, sibling)
        hand.start()
        started.append(hand)
    handed = started[chunks:]
    for c in range(len(turned)):
        turned[c].wait_recv()
        hand = send(piece(theirs + c), piece(theirs + c), 3 * chunks + 1 + c, sibling)
        hand.start()
        handed.append(hand)
    whole.wait_recv()
    own.wait()
    for hand in handed:
        hand.wait_recv()
    for copy in crossing + turned + handed + [whole]:
        copy.wait_send()


def gather(block, spread, chunks, collective_id):
    rows, width = block.shape
    count = 4 * chunks + 1
    return pl.pallas_call(
        functools.partial(gather_kernel, spread, chunks),
        out_shape=jax.ShapeDtypeStruct((4, rows, width), block.dtype),
        in_specs=[pl.BlockSpec(memory_space=pl.ANY)],
        out_specs=pl.BlockSpec(memory_space=pl.ANY),
        scratch_shapes=[
            pltpu.SemaphoreType.DMA((count,)),
            pltpu.SemaphoreType.DMA((count,)),
            pltpu.SemaphoreType.DMA,
        ],
        compiler_params=pltpu.CompilerParams(collective_id=collective_id, has_side_effects=True),
    )(block).reshape(4 * rows, width)


TILE = 16
SLICE = 1536


def total_kernel(pair, lone, x_ref, o_ref, y_got, z_got, z_sent, e_got, send_sem, recv_sem):
    ctx, place = lax.axis_index("ctx"), lax.axis_index("fsdp")
    y = lax.rem(ctx, 2)
    z = ctx // 2
    firsts, lasts = 2 * pair, 2 * lone
    every = firsts + lasts

    def send(src, dst, sem, to_ctx):
        return pltpu.make_async_remote_copy(
            src_ref=src,
            dst_ref=dst,
            send_sem=send_sem.at[sem],
            recv_sem=recv_sem.at[sem],
            device_id=(to_ctx, place),
            device_id_type=MESH_ID,
        )

    y_side = ctx + 1 - 2 * y

    def rows(item, side):
        if item < firsts:
            return pl.ds(pl.multiple_of((side * firsts + item) * TILE, TILE), TILE)
        return pl.ds((firsts + item) * TILE, TILE)

    def end_of(item):
        return item // pair if item < firsts else (item - firsts) // lone

    def turn_of(item):
        return item % pair if item < firsts else (item - firsts) % lone

    def add(store, store_rows, terms):
        @pl.loop(0, x_ref.shape[1] // SLICE)
        def _(i):
            columns = pl.ds(pl.multiple_of(i * SLICE, SLICE), SLICE)
            total = terms[0][0][terms[0][1], columns].astype(jnp.float32)
            for ref, place_rows in terms[1:]:
                total += ref[place_rows, columns].astype(jnp.float32)
            store[store_rows, columns] = total.astype(jnp.bfloat16)

    def slot(item):
        return pl.ds(item * TILE, TILE)

    def pair_copy(item):
        return send(x_ref.at[rows(item, 1 - y), :], y_got.at[slot(item), :], item, y_side)

    def up_copy(item, to_z):
        return send(z_sent.at[slot(item), :], z_got.at[slot(item), :], firsts + item, 2 * to_z + y)

    def end_copy(item):
        return send(
            z_sent.at[slot(item), :],
            e_got.at[slot(item - firsts), :],
            firsts + every + item - firsts,
            y_side,
        )

    def down_copy(item, to_z):
        here = rows(item, y)
        return send(
            o_ref.at[here, :], o_ref.at[here, :], firsts + every + lasts + item, 2 * to_z + y
        )

    def back_copy(item):
        here = rows(item, y)
        return send(
            o_ref.at[here, :], o_ref.at[here, :], firsts + 2 * every + lasts + item, y_side
        )

    barrier = pltpu.get_barrier_semaphore()
    pl.semaphore_signal(barrier, inc=1, device_id=(y_side, place), device_id_type=MESH_ID)

    @pl.when(z > 0)
    def _():
        pl.semaphore_signal(barrier, inc=1, device_id=(ctx - 2, place), device_id_type=MESH_ID)

    @pl.when(z < 3)
    def _():
        pl.semaphore_signal(barrier, inc=1, device_id=(ctx + 2, place), device_id_type=MESH_ID)

    @pl.when((z == 0) | (z == 3))
    def _():
        pl.semaphore_wait(barrier, 2)

    @pl.when((z > 0) & (z < 3))
    def _():
        pl.semaphore_wait(barrier, 3)

    for turn in range(pair):
        for end in range(2):
            pair_copy(end * pair + turn).start()

    def steps(my_z):
        depth = lambda item: 3 - my_z if end_of(item) == 0 else my_z
        toward = lambda item: my_z - 1 if end_of(item) == 0 else my_z + 1
        away = lambda item: my_z + 1 if end_of(item) == 0 else my_z - 1
        events = []
        for item in range(every):
            wait = 1 if item < firsts else 0
            late = 0 if item < firsts else 1
            at = 2 * turn_of(item) + depth(item) + wait
            events.append((at, item, "up"))
            if depth(item) == 3 and late:
                events.append((at + 1, item, "meet"))
            if depth(item) < 3:
                events.append(
                    (2 * turn_of(item) + 3 + wait + late + 3 - depth(item), item, "down")
                )
        pending = []

        def start(copy):
            copy.start()
            pending.append(copy)

        def finish(item):
            if depth(item) > 0:
                start(down_copy(item, away(item)))
            if item < firsts:
                start(back_copy(item))

        for _, item, kind in sorted(events):
            if kind == "up":
                terms = [(x_ref, rows(item, y))]
                if item < firsts:
                    pair_copy(item).wait_recv()
                    terms.append((y_got, slot(item)))
                if depth(item) > 0:
                    up_copy(item, away(item)).wait_recv()
                    terms.append((z_got, slot(item)))
                if depth(item) == 3 and item < firsts:
                    add(o_ref, rows(item, y), terms)
                    finish(item)
                else:
                    add(z_sent, slot(item), terms)
                    if depth(item) == 3:
                        start(end_copy(item))
                    else:
                        start(up_copy(item, toward(item)))
            elif kind == "meet":
                end_copy(item).wait_recv()
                add(
                    o_ref,
                    rows(item, y),
                    [(z_sent, slot(item)), (e_got, slot(item - firsts))],
                )
                finish(item)
            else:
                down_copy(item, toward(item)).wait_recv()
                finish(item)
        for copy in pending:
            copy.wait_send()

    for my_z in range(4):
        pl.when(z == my_z)(functools.partial(steps, my_z))

    for item in range(firsts):
        pair_copy(item).wait_send()
        send(
            o_ref.at[rows(item, y), :],
            o_ref.at[rows(item, 1 - y), :],
            firsts + 2 * every + lasts + item,
            y_side,
        ).wait_recv()


def total_over_ctx(grads, collective_id):
    rows, width = grads.shape
    chunks = rows // TILE
    pair, lone = chunks // 8, chunks // 4
    items = 2 * pair + 2 * lone
    sems = 4 * pair + 2 * items + 2 * lone
    low = lambda count: pltpu.VMEM((count * TILE, width), jnp.bfloat16)
    return pl.pallas_call(
        functools.partial(total_kernel, pair, lone),
        out_shape=jax.ShapeDtypeStruct((rows, width), jnp.bfloat16),
        in_specs=[pl.BlockSpec(memory_space=pltpu.VMEM)],
        out_specs=pl.BlockSpec(memory_space=pltpu.VMEM),
        scratch_shapes=[
            low(2 * pair),
            low(items),
            low(items),
            low(2 * lone),
            pltpu.SemaphoreType.DMA((sems,)),
            pltpu.SemaphoreType.DMA((sems,)),
        ],
        compiler_params=pltpu.CompilerParams(
            collective_id=collective_id,
            has_side_effects=True,
            vmem_limit_bytes=48 * 1024 * 1024,
        ),
    )(grads)


def pack(blocks):
    half = blocks.shape[-2] // 2
    return jnp.concatenate([blocks[..., :half, :], blocks[..., half:, :]], axis=-1)


def unpack(blocks):
    half = blocks.shape[-1] // 2
    return jnp.concatenate([blocks[..., :half], blocks[..., half:]], axis=-2)


CONTRACT_LAST = (((1,), (1,)), ((), ()))
CONTRACT_FIRST = (((0,), (0,)), ((), ()))


def attend_kernel(q_ref, k_ref, v_ref, context_ref, log_ref):
    scores = lax.dot_general(
        q_ref[...], k_ref[...], CONTRACT_LAST, preferred_element_type=jnp.float32
    )
    top = jnp.max(scores, axis=-1, keepdims=True)
    weights = jnp.exp(scores - top)
    total = jnp.sum(weights, axis=-1, keepdims=True)
    weighted = jnp.dot(
        weights.astype(jnp.bfloat16), v_ref[...], preferred_element_type=jnp.float32
    )
    context_ref[...] = weighted / total
    log_ref[...] = top + jnp.log(total)


def attend(queries, key_rows, value_rows, block):
    rows, size = queries.shape
    return pl.pallas_call(
        attend_kernel,
        grid=(rows // block,),
        out_shape=(
            jax.ShapeDtypeStruct((rows, size), jnp.float32),
            jax.ShapeDtypeStruct((rows, 1), jnp.float32),
        ),
        in_specs=[
            pl.BlockSpec((block, size), lambda i: (i, 0)),
            pl.BlockSpec((rows, size), lambda i: (0, 0)),
            pl.BlockSpec((rows, size), lambda i: (0, 0)),
        ],
        out_specs=(
            pl.BlockSpec((block, size), lambda i: (i, 0)),
            pl.BlockSpec((block, 1), lambda i: (i, 0)),
        ),
        compiler_params=pltpu.CompilerParams(vmem_limit_bytes=48 * 1024 * 1024),
    )(queries, key_rows, value_rows)


def attend_back_kernel(
    q_ref, k_ref, v_ref, context_ref, log_ref, grad_ref, dq_ref, dk_ref, dv_ref
):
    @pl.when(pl.program_id(0) == 0)
    def _():
        dk_ref[...] = jnp.zeros_like(dk_ref)
        dv_ref[...] = jnp.zeros_like(dv_ref)

    grad = grad_ref[...]
    inner = jnp.sum(grad.astype(jnp.float32) * context_ref[...], axis=-1, keepdims=True)
    scores = lax.dot_general(
        q_ref[...], k_ref[...], CONTRACT_LAST, preferred_element_type=jnp.float32
    )
    probs = jnp.exp(scores - log_ref[...])
    prob_grad = lax.dot_general(
        grad, v_ref[...], CONTRACT_LAST, preferred_element_type=jnp.float32
    )
    score_grad = (probs * (prob_grad - inner)).astype(jnp.bfloat16)
    dv_ref[...] += lax.dot_general(
        probs.astype(jnp.bfloat16), grad, CONTRACT_FIRST, preferred_element_type=jnp.float32
    )
    dk_ref[...] += lax.dot_general(
        score_grad, q_ref[...], CONTRACT_FIRST, preferred_element_type=jnp.float32
    )
    dq_ref[...] = jnp.dot(score_grad, k_ref[...], preferred_element_type=jnp.float32)


def attend_back(queries, key_rows, value_rows, context, log_total, grad, block):
    rows, size = queries.shape
    part = pl.BlockSpec((block, size), lambda i: (i, 0))
    whole = pl.BlockSpec((rows, size), lambda i: (0, 0))
    return pl.pallas_call(
        attend_back_kernel,
        grid=(rows // block,),
        out_shape=(jax.ShapeDtypeStruct((rows, size), jnp.float32),) * 3,
        in_specs=[
            part,
            whole,
            whole,
            part,
            pl.BlockSpec((block, 1), lambda i: (i, 0)),
            part,
        ],
        out_specs=(part, whole, whole),
        compiler_params=pltpu.CompilerParams(vmem_limit_bytes=48 * 1024 * 1024),
    )(queries, key_rows, value_rows, context, log_total, grad)


def by_head_forward(mixed_rows, cos_table, sin_table, scaling):
    seq_count, row_count, _, head_count, head_size = mixed_rows.shape
    ctx_count, fsdp_count = lax.axis_size("ctx"), lax.axis_size("fsdp")
    count = ctx_count * fsdp_count
    queries = rotate(mixed_rows[:, :, 0], cos_table, sin_table).astype(jnp.bfloat16) * scaling
    key_rows = rotate(mixed_rows[:, :, 1], cos_table, sin_table).astype(jnp.bfloat16)
    value_rows = mixed_rows[:, :, 2].astype(jnp.bfloat16)
    to_head = lambda rows: rows.transpose(0, 2, 1, 3).reshape(count, row_count, head_size)
    sent = jnp.concatenate(
        [
            jnp.concatenate([to_head(queries), to_head(key_rows)], axis=-1),
            pack(to_head(value_rows)),
        ],
        axis=1,
    )
    got = exchange(sent, ctx_count, fsdp_count, 1)
    flat = lambda rows: rows.reshape(count * row_count, head_size)
    queries = flat(got[:, :row_count, :head_size])
    key_rows = flat(got[:, :row_count, head_size:])
    value_rows = flat(unpack(got[:, row_count:]))
    context, log_total = attend(queries, key_rows, value_rows, 256)
    back = exchange(
        pack(context.astype(jnp.bfloat16).reshape(count, row_count, head_size)),
        ctx_count,
        fsdp_count,
        2,
    )
    context_low = (
        unpack(back)
        .reshape(seq_count, head_count, row_count, head_size)
        .transpose(0, 2, 1, 3)
        .reshape(seq_count * row_count, head_count * head_size)
    )
    return context_low, (queries, key_rows, value_rows, context, log_total)


def by_head_back(context_grad, saved, scaling, after):
    seq_count, row_count, head_count, head_size = context_grad.shape
    ctx_count, fsdp_count = lax.axis_size("ctx"), lax.axis_size("fsdp")
    count = ctx_count * fsdp_count
    queries, key_rows, value_rows, context, log_total = saved
    sent = pack(context_grad.transpose(0, 2, 1, 3).reshape(count, row_count, head_size))
    grad = unpack(exchange(sent, ctx_count, fsdp_count, 3)).reshape(count * row_count, head_size)
    query_grad, key_grad, value_grad = attend_back(
        queries, key_rows, value_rows, context, log_total, grad, 256
    )
    cos_all, sin_all = angles(jnp.arange(count * row_count, dtype=jnp.int32), head_size)
    cos_all, sin_all = cos_all[:, 0], sin_all[:, 0]
    query_pre = unrotate(query_grad * scaling, cos_all, sin_all).astype(jnp.bfloat16)
    key_pre = unrotate(key_grad, cos_all, sin_all).astype(jnp.bfloat16)
    split = lambda rows: rows.reshape(count, row_count, head_size)
    sent = jnp.concatenate(
        [
            jnp.concatenate([split(query_pre), split(key_pre)], axis=-1),
            pack(split(value_grad.astype(jnp.bfloat16))),
        ],
        axis=1,
    )
    sent, after = lax.optimization_barrier((sent, after))
    got = exchange(sent, ctx_count, fsdp_count, 4)
    parts = jnp.stack(
        [got[:, :row_count, :head_size], got[:, :row_count, head_size:], unpack(got[:, row_count:])]
    )
    return (
        parts.reshape(3, seq_count, head_count, row_count, head_size)
        .transpose(1, 3, 0, 2, 4)
        .reshape(seq_count * row_count, 3 * head_count * head_size)
    ), after


def by_block_forward(mixed_rows, cos_table, sin_table, scaling):
    seq_count, row_count, _, head_count, head_size = mixed_rows.shape
    width = head_count * head_size
    queries = rotate(mixed_rows[:, :, 0], cos_table, sin_table).astype(jnp.bfloat16)
    key_flat = (
        rotate(mixed_rows[:, :, 1], cos_table, sin_table)
        .astype(jnp.bfloat16)
        .reshape(seq_count, row_count, width)
    )
    value_flat = mixed_rows[:, :, 2].astype(jnp.bfloat16).reshape(seq_count, row_count, width)
    key_block, value_block = (
        lax.all_gather(key_flat, "fsdp", axis=1, tiled=True),
        lax.all_gather(value_flat, "fsdp", axis=1, tiled=True),
    )
    start_state = empty_state(seq_count, head_count, row_count, head_size)
    running_max, denominator, weighted = forward_step(
        queries,
        scaling,
        start_state,
        (
            lax.all_gather(key_block, "ctx", axis=1, tiled=True),
            lax.all_gather(value_block, "ctx", axis=1, tiled=True),
        ),
    )
    context = (weighted / denominator[..., None]).transpose(0, 2, 1, 3)
    log_total = running_max + jnp.log(denominator)
    context_low = context.reshape(seq_count * row_count, width).astype(jnp.bfloat16)
    return context_low, (queries, key_block, value_block, context, log_total, cos_table, sin_table)


def by_block_back(context_grad, saved, scaling, after):
    seq_count, row_count, head_count, head_size = context_grad.shape
    width = head_count * head_size
    queries, key_block, value_block, context, log_total, cos_table, sin_table = saved
    inner = jnp.sum(context_grad.astype(jnp.float32) * context, axis=-1)
    inner_heads = inner.transpose(0, 2, 1)
    log_rows = log_total.transpose(0, 2, 1)
    query_grad = query_step(
        queries,
        context_grad,
        log_total,
        inner_heads,
        scaling,
        (
            lax.all_gather(key_block, "ctx", axis=1, tiled=True),
            lax.all_gather(value_block, "ctx", axis=1, tiled=True),
        ),
    )
    block_len = key_block.shape[1]
    query_wide = queries.reshape(seq_count, row_count, width).astype(jnp.float32)
    grad_wide = context_grad.reshape(seq_count, row_count, width).astype(jnp.float32)
    key_grad, value_grad = key_step(
        as_heads(key_block, head_size),
        as_heads(value_block, head_size),
        scaling,
        (
            lax.all_gather(query_wide, "ctx", axis=1, tiled=True),
            lax.all_gather(grad_wide, "ctx", axis=1, tiled=True),
            lax.all_gather(log_rows, "ctx", axis=1, tiled=True),
            lax.all_gather(inner, "ctx", axis=1, tiled=True),
        ),
    )
    own = lambda grad: lax.psum_scatter(
        grad.reshape(seq_count, block_len, width), "fsdp", scatter_dimension=1, tiled=True
    ).reshape(seq_count, row_count, head_count, head_size)
    query_pre = unrotate(query_grad * scaling, cos_table, sin_table)
    key_pre = unrotate(own(key_grad) * scaling, cos_table, sin_table)
    return (
        jnp.stack([query_pre, key_pre, own(value_grad)], axis=2)
        .reshape(seq_count * row_count, 3 * width)
        .astype(jnp.bfloat16)
    ), after


def group_rows(rows):
    return lax.all_gather(rows, "fsdp", axis=0, tiled=True)


def group_columns(arrays):
    count = lax.axis_size("fsdp")
    widths = [rows.shape[1] // count for rows in arrays]
    sent = jnp.stack(
        [
            jnp.concatenate(
                [rows[:, f * width : (f + 1) * width] for rows, width in zip(arrays, widths)],
                axis=1,
            )
            for f in range(count)
        ]
    )
    got = lax.all_to_all(sent, "fsdp", split_axis=0, concat_axis=0, tiled=True)
    got = got.reshape(-1, sum(widths))
    edges = [sum(widths[:i]) for i in range(len(widths) + 1)]
    return [got[:, edges[i] : edges[i + 1]] for i in range(len(widths))]


def weight_grad(left, right):
    return jnp.einsum("tw,tf->wf", left, right, preferred_element_type=jnp.float32)


def on_device(inputs, attn_gain, attn_proj, attn_out, mlp_gain, mlp_in, mlp_out, cotangent):
    seq_count, row_count, model_width = inputs.shape
    head_size = HEAD_DIM
    head_count = HEADS
    scaling = head_size ** (-0.5)
    fsdp_count = lax.axis_size("fsdp")
    fsdp_place = lax.axis_index("fsdp")
    device_count = lax.axis_size("ctx") * fsdp_count
    one_head_each = device_count == seq_count * head_count
    start_row = (lax.axis_index("ctx") * fsdp_count + fsdp_place) * row_count
    cos_table, sin_table = angles(start_row + jnp.arange(row_count, dtype=jnp.int32), head_size)
    tokens = seq_count * row_count
    gain_width = own_rows = attn_gain.shape[0]
    gains = lax.all_gather(jnp.stack([attn_gain, mlp_gain]), "fsdp", axis=1, tiled=True).astype(
        jnp.float32
    )
    gain_one, gain_two = gains[0], gains[1]
    ctx_count = lax.axis_size("ctx")
    small = one_head_each and fsdp_count == 4 and ctx_count == 8
    proj_full, out_full, lift_full, down_full = (
        gather(attn_proj, True, 3, 6)
        if small
        else lax.all_gather(attn_proj, "fsdp", axis=0, tiled=True),
        lax.all_gather(attn_out, "fsdp", axis=0, tiled=True),
        lax.all_gather(mlp_in, "fsdp", axis=0, tiled=True),
        lax.all_gather(mlp_out, "fsdp", axis=0, tiled=True),
    )
    states = inputs.astype(jnp.float32)
    normed, norm_back_one = jax.vjp(layer_norm, states, gain_one)
    normed_low = normed.astype(jnp.bfloat16).reshape(tokens, model_width)
    mixed_rows = jnp.dot(normed_low, proj_full, preferred_element_type=jnp.float32).reshape(
        seq_count, row_count, 3, head_count, head_size
    )
    attention, attention_back = (
        (by_head_forward, by_head_back) if one_head_each else (by_block_forward, by_block_back)
    )
    context_low, saved = attention(mixed_rows, cos_table, sin_table, scaling)
    branch = jnp.dot(context_low, out_full, preferred_element_type=jnp.float32).reshape(
        seq_count, row_count, model_width
    )
    middle = states + branch
    normed_two, norm_back_two = jax.vjp(layer_norm, middle, gain_two)
    normed_two_low = normed_two.astype(jnp.bfloat16).reshape(tokens, model_width)
    lifted = jnp.dot(normed_two_low, lift_full, preferred_element_type=jnp.float32)
    gate_out, gated_back = jax.vjp(gated_unit, lifted)
    gate_low = gate_out.astype(jnp.bfloat16)
    outputs = (
        middle
        + jnp.dot(gate_low, down_full, preferred_element_type=jnp.float32).reshape(
            seq_count, row_count, model_width
        )
    ).astype(jnp.bfloat16)
    seed_rows = cotangent.reshape(tokens, model_width)
    gate_grad = jnp.einsum("td,fd->tf", seed_rows, down_full, preferred_element_type=jnp.float32)
    lifted_grad = gated_back(gate_grad)[0].astype(jnp.bfloat16)
    normed_two_grad = jnp.einsum(
        "tf,wf->tw", lifted_grad, lift_full, preferred_element_type=jnp.float32
    ).reshape(seq_count, row_count, model_width)
    middle_part, gain_two_grad = norm_back_two(normed_two_grad)
    middle_grad = cotangent.astype(jnp.float32) + middle_part
    middle_low = middle_grad.reshape(tokens, model_width).astype(jnp.bfloat16)
    context_grad = (
        jnp.einsum("tv,wv->tw", middle_low, out_full, preferred_element_type=jnp.float32)
        .astype(jnp.bfloat16)
        .reshape(seq_count, row_count, head_count, head_size)
    )
    normed_two_part, gate_part, context_part, normed_part = group_columns(
        (normed_two_low, gate_low, context_low, normed_low)
    )
    seed_group = group_rows(seed_rows)
    joined = group_rows(jnp.concatenate([lifted_grad, middle_low], axis=1))
    lift_grad = weight_grad(normed_two_part, joined[:, : lifted_grad.shape[1]])
    out_grad = weight_grad(context_part, joined[:, lifted_grad.shape[1] :])
    down_grad = weight_grad(gate_part, seed_group)
    first_grads = tuple(grad.astype(jnp.bfloat16) for grad in (lift_grad, down_grad, out_grad))
    mixed_grad, first_grads = attention_back(context_grad, saved, scaling, first_grads)
    normed_grad = jnp.einsum(
        "tm,wm->tw", mixed_grad, proj_full, preferred_element_type=jnp.float32
    ).reshape(seq_count, row_count, model_width)
    state_part, gain_one_grad = norm_back_one(normed_grad)
    input_grad = middle_grad + state_part
    mixed_group = gather(mixed_grad, False, 4, 7) if small else group_rows(mixed_grad)
    proj_grad = weight_grad(normed_part, mixed_group).astype(jnp.bfloat16)
    grads = (*first_grads, proj_grad)
    if small:
        sheet = [grad.reshape(own_rows, -1) for grad in grads]
        widths = [grad.shape[1] for grad in sheet]
        spare = -sum(widths) % SLICE
        sheet = jnp.concatenate(
            [sheet[0], sheet[2], sheet[3], sheet[1], jnp.zeros((own_rows, spare), jnp.bfloat16)],
            axis=1,
        )
        sums = total_over_ctx(sheet, 8)
        edges = [0, widths[0], widths[0] + widths[2], widths[0] + widths[2] + widths[3]]
        lift_sum, out_sum, proj_sum, down_sum = (
            sums[:, edges[0] : edges[1]],
            sums[:, edges[1] : edges[2]],
            sums[:, edges[2] : edges[3]],
            sums[:, edges[3] : edges[3] + widths[1]].reshape(mlp_out.shape),
        )
    else:
        lift_sum, down_sum, out_sum, proj_sum = lax.psum(grads, "ctx")
    lift_sum, down_sum, out_sum, proj_sum = (
        total.astype(jnp.float32) for total in (lift_sum, down_sum, out_sum, proj_sum)
    )
    gain_grads = jnp.stack([gain_one_grad, gain_two_grad])
    if small:
        shares = gain_grads.reshape(2, fsdp_count, gain_width).transpose(1, 0, 2)
        shares = jnp.concatenate([shares, jnp.zeros((fsdp_count, 6, gain_width))], axis=1)
        shares = jnp.concatenate([shares] * ctx_count, axis=0)
        gain_own = jnp.sum(exchange(shares, ctx_count, fsdp_count, 5), axis=0)
    else:
        gain_sums = lax.psum(gain_grads, ("ctx", "fsdp"))
        gain_own = lax.dynamic_slice_in_dim(gain_sums, fsdp_place * gain_width, gain_width, axis=1)
    return (
        outputs,
        input_grad,
        gain_own[0],
        proj_sum,
        out_sum,
        gain_own[1],
        lift_sum,
        down_sum,
    )


def solution(mesh):
    in_specs = (
        P(None, ("ctx", "fsdp"), None),
        P("fsdp"),
        P("fsdp", None),
        P("fsdp", None),
        P("fsdp"),
        P("fsdp", None),
        P("fsdp", None),
        P(None, ("ctx", "fsdp"), None),
    )
    out_specs = (
        P(None, ("ctx", "fsdp"), None),
        P(None, ("ctx", "fsdp"), None),
        P("fsdp"),
        P("fsdp", None),
        P("fsdp", None),
        P("fsdp"),
        P("fsdp", None),
        P("fsdp", None),
    )
    return jax.shard_map(
        on_device, mesh=mesh, in_specs=in_specs, out_specs=out_specs, check_vma=False
    )
```
